512 devices in a mesh: dp: 256 (over x, z, y_hi, core), pair: 2 (over y_lo).
Axes of the slice: x: 4, y: 4 (y_hi: 2, y_lo: 2; y = y_hi * 2 + y_lo), z: 16, core: 2. Of those that a mesh axis runs over, the one named last changes fastest.
Arguments:
- picture_features: float32 [131072, 1152], P(('dp', 'pair')), may hold values from -0.18 to 0.18
- caption_features: float32 [131072, 1152], P('dp'), may hold values from -0.18 to 0.18
- sharpness_factor: float32 [1], replicated, may hold values from 20 to 40
- score_intercept: float32 [1], replicated, may hold values from -4 to -1
Outputs:
- image_grad: float32 [131072, 1152], P(('dp', 'pair'))
- text_grad: float32 [131072, 1152], P(('dp', 'pair'))
The draws below stay inside these ranges and needn't reach their ends.
All inputs are finite; a program needn't handle non-finite values.
Results may differ from the reference program's by a relative error of at most 0.0003.
Values sent between devices are 32-bit elements; how exact they have to be, the bound alone decides.
A program may use at most 64 MiB of HBM per device.

```python
import jax
import jax.numpy as jnp
from jax import lax

D = 1152
TXT_DEV = 512
WINDOW = 4
BATCH = 131072
N_DP = 256


def steps_of(key, shape, pieces, smallest, top_value):
    gain, own = 1.0, jax.random.fold_in(key, 6)
    for axis_at, parts in pieces:
        steps = jnp.exp(jax.random.uniform(jax.random.fold_in(own, axis_at), (parts,), jnp.float32, smallest / len(pieces), top_value / len(pieces)))
        gain = gain * jnp.repeat(steps, shape[axis_at] // parts).reshape([-1 if axis == axis_at else 1 for axis in range(len(shape))])
    return gain


def noise(own_key, shape, spread, limit, shards=(), kind=jnp.bfloat16):
    entries = spread * jax.random.normal(own_key, shape, jnp.float32)
    if shards:
        entries = entries * steps_of(own_key, shape, shards, -0.22, 0.18)
    return jnp.clip(entries, -limit, limit).astype(kind)


def setup_inputs(seed: int = 0) -> dict:
    streams_of = jax.random.split(jax.random.key(seed), 5)
    picture_features = noise(streams_of[0], (BATCH, D), 0.03, 0.18, ((0, 512),), jnp.float32)
    caption_features = noise(streams_of[1], (BATCH, D), 0.03, 0.18, ((0, 256),), jnp.float32)
    sharpness_factor = jnp.clip(jax.random.uniform(streams_of[2], (1,), jnp.float32, 20.0, 40.0), 20.0, 40.0)
    score_intercept = jnp.clip(jax.random.uniform(streams_of[3], (1,), jnp.float32, -4.0, -1.0), -4.0, -1.0)
    return dict(picture_features=picture_features, caption_features=caption_features, sharpness_factor=sharpness_factor, score_intercept=score_intercept)


def reference(picture_features, caption_features, sharpness_factor, score_intercept):
    count = N_DP
    rows = TXT_DEV
    similarity_multiplier = sharpness_factor[0]
    diagonal_displacement = score_intercept[0]
    images = picture_features.reshape(count, rows, D)
    texts = caption_features.reshape(count, rows, D)
    labels = 2.0 * jnp.eye(rows, dtype=jnp.float32) - 1.0
    high = lax.Precision.HIGHEST

    def block(text_accumulator, index):
        image_rows = images[index]
        grad_rows = jnp.zeros((rows, D), jnp.float32)
        for step in range(WINDOW):
            other = ((index - step) % count).astype(jnp.int32)
            partner = lax.dynamic_index_in_dim(texts, other, 0, keepdims=False)
            similarity_matrix = similarity_multiplier * jnp.dot(image_rows, partner.T, precision=high) + diagonal_displacement
            sign = labels if step == 0 else -jnp.ones((rows, rows), jnp.float32)
            coef = -sign * jax.nn.sigmoid(-sign * similarity_matrix)
            grad_rows = grad_rows + similarity_multiplier * jnp.dot(coef, partner, precision=high)
            term = similarity_multiplier * jnp.dot(coef.T, image_rows, precision=high)
            active_slice = lax.dynamic_index_in_dim(text_accumulator, other, 0, keepdims=False)
            text_accumulator = lax.dynamic_update_index_in_dim(text_accumulator, active_slice + term, other, 0)
        return text_accumulator, grad_rows

    start = jnp.zeros((count, rows, D), jnp.float32)
    text_accumulator, image_grads = lax.scan(block, start, jnp.arange(count, dtype=jnp.int32))
    return image_grads.reshape(count * rows, D), text_accumulator.reshape(count * rows, D)
```

```python
import functools

import jax
import jax.numpy as jnp
from jax import lax
from jax.experimental import pallas as pl
from jax.experimental.pallas import tpu as pltpu
from jax.sharding import PartitionSpec as P

MESH = pl.DeviceIdType.MESH
F32, BF16 = jnp.float32, jnp.bfloat16
CHUNK = 64
OWN_CHUNK = 128


def halves(value):
    high = value.astype(BF16)
    return high, (value - high.astype(F32)).astype(BF16)


def dot(a, b):
    return jnp.dot(a, b, preferred_element_type=F32)


def kernel(
    n, scale_ref, bias_ref, pic, cap, image_out, text_out,
    img, text, t_high, t_low, tt_high, tt_low, grad, text_grad,
    part, ret, ret_far, text_ret,
    load_sem, out_sem, s1, s2, s3, sf, sp, sr, sx, st, r1, r2, r3, rp, rr, rx, rt,
):
    dp, p = lax.axis_index("dp"), lax.axis_index("pair")
    half, words = pic.shape[0], cap.shape[0]
    chunks = half // CHUNK
    core = lax.rem(dp, 2)
    low = lax.rem(dp, 4) < 2
    a0 = low & (core == 0)
    a1 = low & (core == 1)
    b0 = jnp.logical_not(low) & (core == 0)

    def there(step, row):
        return (lax.rem(dp + step + n, n), row)

    q = 1 - p
    sibling = there(1 - 2 * core, p)
    down, up = there(-2, q), there(2, q)
    across = there(jnp.where(core == 1, 1, -1), q)
    far = there(jnp.where(core == 1, 3, -3), p)
    first_to = there(jnp.where(core == 1, -1, -3), p)
    first_back = there(jnp.where(core == 1, 3, 1), p)
    partner = (dp, q)
    main, other = 2 + core, 3 - core

    def rows(k, size=CHUNK):
        return pl.ds(pl.multiple_of(k * size, size), size)

    def remote(src, dst, send, recv, device):
        return pltpu.make_async_remote_copy(
            src_ref=src, dst_ref=dst, send_sem=send, recv_sem=recv, device_id=device, device_id_type=MESH
        )

    def each(body, count=chunks):
        def run(k, _):
            body(k)
            return 0

        lax.fori_loop(0, count, run, 0)

    def send_main(k):
        return remote(pic.at[rows(k)], img.at[main, rows(k)], s2.at[k], r2.at[k], down)

    def send_first(k):
        return remote(pic.at[rows(k)], img.at[1, rows(k)], s1.at[k], r1.at[k], first_to)

    def forward_first(k):
        return remote(img.at[1, rows(k)], img.at[2, rows(k)], sf.at[k], r2.at[k], across)

    def forward_main(k):
        return remote(img.at[main, rows(k)], img.at[main, rows(k)], s3.at[k], r3.at[k], sibling)

    def send_part(k):
        return remote(grad.at[other, rows(k)], part.at[rows(k)], sp.at[k], rp.at[k], sibling)

    def send_first_back(k):
        return remote(grad.at[1, rows(k)], ret_far.at[rows(k)], sx.at[k], rx.at[k], first_back)

    to_across = jnp.where(b0, 1, 0)
    back = tuple(jnp.where(b0, x, y) for x, y in zip(across, up, strict=True))

    def send_main_back(k):
        return remote(
            grad.at[main, rows(k)], ret.at[to_across, rows(k)], sr.at[k], rr.at[to_across, k], back
        )

    def get_back(which, k):
        return remote(grad.at[main, rows(k)], ret.at[which, rows(k)], sr.at[k], rr.at[which, k], back)

    def send_text(k):
        return remote(
            text_grad.at[rows(q * chunks + k)], text_ret.at[rows(k)], st.at[k], rt.at[k], partner
        )

    load_own = pltpu.make_async_copy(pic, img.at[0], load_sem.at[0])
    load_text = pltpu.make_async_copy(cap, text, load_sem.at[1])
    load_text.start()
    load_own.start()

    barrier = pltpu.get_barrier_semaphore()
    for device in (sibling, down, up, across, far, partner):
        pl.semaphore_signal(barrier, inc=1, device_id=device, device_id_type=MESH)
    pl.semaphore_wait(barrier, 6)

    @pl.loop(0, chunks)
    def _(k):
        send_first(k).start()

        @pl.when(jnp.logical_not(a0))
        def _():
            send_main(k).start()

    scale, bias = scale_ref[0], bias_ref[0]
    load_text.wait()
    high, lower = halves(text[...])
    t_high[...] = high
    t_low[...] = lower
    tt_high[...] = high.T
    tt_low[...] = lower.T
    text_grad[...] = jnp.zeros_like(text_grad)
    load_own.wait()

    def score(slot, k, size, own):
        i_high, i_low = halves(img[slot, rows(k, size)])
        both = dot(jnp.concatenate([i_high, i_low], 0), tt_high[...])
        logits = scale * (both[:size] + both[size:] + dot(i_high, tt_low[...])) + bias
        if own:
            row = lax.broadcasted_iota(jnp.int32, logits.shape, 0) + (p * half + k * size)
            sign = jnp.where(row == lax.broadcasted_iota(jnp.int32, logits.shape, 1), -1.0, 1.0)
            coef = sign * jax.nn.sigmoid(sign * logits)
        else:
            coef = jax.nn.sigmoid(logits)
        c_high, c_low = halves(scale * coef)
        both = dot(jnp.concatenate([c_high, c_low], 0), t_high[...])
        grad[slot, rows(k, size)] = both[:size] + both[size:] + dot(c_high, t_low[...])
        text_grad[...] += lax.dot_general(
            jnp.concatenate([c_high, c_low, c_high], 0),
            jnp.concatenate([i_high, i_high, i_low], 0),
            (((0,), (0,)), ((), ())),
            preferred_element_type=F32,
        )

    @pl.loop(0, half // OWN_CHUNK)
    def _(k):
        score(0, k, OWN_CHUNK, True)

    @pl.loop(0, chunks)
    def _(k):
        send_first(k).wait_recv()

        @pl.when(a1)
        def _():
            forward_first(k).start()

        score(1, k, CHUNK, False)

        @pl.when(jnp.logical_not(a1))
        def _():
            send_first_back(k).start()

        send_main(k).wait_recv()
        forward_main(k).start()
        score(main, k, CHUNK, False)
        forward_main(k).wait_recv()
        score(other, k, CHUNK, False)
        send_part(k).start()

    @pl.loop(0, chunks)
    def _(k):
        send_text(k).start()
        send_part(k).wait_recv()
        grad[main, rows(k)] += part[rows(k)]
        send_main_back(k).start()

    @pl.loop(0, chunks)
    def _(k):
        @pl.when(a1)
        def _():
            get_back(1, k).wait_recv()
            grad[1, rows(k)] += ret[1, rows(k)]
            send_first_back(k).start()

        @pl.when(jnp.logical_not(a0))
        def _():
            get_back(0, k).wait_recv()
            grad[0, rows(k)] += ret[0, rows(k)]

        send_text(k).wait_recv()
        text_grad[rows(p * chunks + k)] += text_ret[rows(k)]
        pltpu.make_async_copy(
            text_grad.at[rows(p * chunks + k)], text_out.at[rows(k)], out_sem.at[0, k]
        ).start()
        send_first_back(k).wait_recv()
        grad[0, rows(k)] += ret_far[rows(k)]
        pltpu.make_async_copy(grad.at[0, rows(k)], image_out.at[rows(k)], out_sem.at[1, k]).start()

    @pl.loop(0, chunks)
    def _(k):
        send_first(k).wait_send()

        @pl.when(jnp.logical_not(a0))
        def _():
            send_main(k).wait_send()

        @pl.when(a1)
        def _():
            forward_first(k).wait_send()

        forward_main(k).wait_send()
        send_part(k).wait_send()
        send_main_back(k).wait_send()
        send_first_back(k).wait_send()
        send_text(k).wait_send()
        pltpu.make_async_copy(
            text_grad.at[rows(p * chunks + k)], text_out.at[rows(k)], out_sem.at[0, k]
        ).wait()
        pltpu.make_async_copy(grad.at[0, rows(k)], image_out.at[rows(k)], out_sem.at[1, k]).wait()


def solution(mesh):
    n = mesh.shape["dp"]

    def shards(picture_features, caption_features, sharpness_factor, score_intercept):
        half, width = picture_features.shape
        words = caption_features.shape[0]
        chunks = half // CHUNK
        dma = pltpu.SemaphoreType.DMA
        return pl.pallas_call(
            functools.partial(kernel, n),
            name="window_grads",
            out_shape=[jax.ShapeDtypeStruct((half, width), F32)] * 2,
            in_specs=[pl.BlockSpec(memory_space=pltpu.SMEM)] * 2 + [pl.BlockSpec(memory_space=pl.ANY)] * 2,
            out_specs=[pl.BlockSpec(memory_space=pl.ANY)] * 2,
            scratch_shapes=[
                pltpu.VMEM((4, half, width), F32),
                pltpu.VMEM((words, width), F32),
                pltpu.VMEM((words, width), BF16),
                pltpu.VMEM((words, width), BF16),
                pltpu.VMEM((width, words), BF16),
                pltpu.VMEM((width, words), BF16),
                pltpu.VMEM((4, half, width), F32),
                pltpu.VMEM((words, width), F32),
                pltpu.VMEM((half, width), F32),
                pltpu.VMEM((2, half, width), F32),
                pltpu.VMEM((half, width), F32),
                pltpu.VMEM((half, width), F32),
                dma((2,)),
                dma((2, chunks)),
            ]
            + [dma((chunks,))] * 12
            + [dma((2, chunks)), dma((chunks,)), dma((chunks,))],
            compiler_params=pltpu.CompilerParams(
                collective_id=0, has_side_effects=True, vmem_limit_bytes=48 * 2**20
            ),
            cost_estimate=pl.CostEstimate(
                flops=4 * 3 * 2 * half * words * width, bytes_accessed=4 * width * (3 * half + words), transcendentals=0
            ),
        )(sharpness_factor, score_intercept, picture_features, caption_features)

    return jax.shard_map(
        shards,
        mesh=mesh,
        in_specs=(P(("dp", "pair"), None), P("dp", None), P(), P()),
        out_specs=(P(("dp", "pair"), None), P(("dp", "pair"), None)),
        check_vma=False,
    )
```

```python
import functools

import jax
import jax.numpy as jnp
from jax import lax
from jax.experimental import pallas as pl
from jax.experimental.pallas import tpu as pltpu
from jax.sharding import PartitionSpec as P

MESH = pl.DeviceIdType.MESH
F32, BF16 = jnp.float32, jnp.bfloat16
CHUNK = 64


def halves(value):
    high = value.astype(BF16)
    return high, (value - high.astype(F32)).astype(BF16)


def dot(a, b):
    return jnp.dot(a, b, preferred_element_type=F32)


def kernel(
    n, scale_ref, bias_ref, pic, cap, image_out, text_out,
    img, text, t_high, t_low, tt_high, tt_low, grad, text_grad,
    part, ret, ret_far, text_ret, stage, stage_back,
    load_sem, out_sem, s1, s2, s3, sf, sp, sr, sx, st, sg, sb, r1, r2, r3, rp, rg, rb, rr, rx, rt, ready,
):
    dp, p = lax.axis_index("dp"), lax.axis_index("pair")
    half, words = pic.shape[0], cap.shape[0]
    chunks = half // CHUNK
    core = lax.rem(dp, 2)
    low = lax.rem(dp, 4) < 2
    a0 = low & (core == 0)
    a1 = low & (core == 1)
    b0 = jnp.logical_not(low) & (core == 0)
    b1 = jnp.logical_not(low) & (core == 1)

    def there(step, row):
        return (lax.rem(dp + step + n, n), row)

    q = 1 - p
    sibling = there(1 - 2 * core, p)
    down, up = there(-2, q), there(2, q)
    across = there(jnp.where(core == 1, 1, -1), q)
    far = there(jnp.where(core == 1, 3, -3), p)
    first_to = there(jnp.where(core == 1, -1, -3), p)
    first_back = there(jnp.where(core == 1, 3, 1), p)
    partner = (dp, q)
    main, other = 2 + core, 3 - core
    next_up, next_down = there(4, p), there(-4, p)

    def rows(k, size=CHUNK):
        return pl.ds(pl.multiple_of(k * size, size), size)

    def remote(src, dst, send, recv, device):
        return pltpu.make_async_remote_copy(
            src_ref=src, dst_ref=dst, send_sem=send, recv_sem=recv, device_id=device, device_id_type=MESH
        )

    def each(body, count=chunks):
        def run(k, _):
            body(k)
            return 0

        lax.fori_loop(0, count, run, 0)

    def send_main(k):
        return remote(pic.at[rows(k)], img.at[main, rows(k)], s2.at[k], r2.at[k], down)

    def send_first(k):
        return remote(pic.at[rows(k)], img.at[1, rows(k)], s1.at[k], r1.at[k], first_to)

    def forward_first(k):
        return remote(img.at[1, rows(k)], img.at[other, rows(k)], sf.at[k], r2.at[k], across)

    def send_stage(k):
        return remote(pic.at[rows(k)], stage.at[rows(k)], s2.at[k], rg.at[k], up)

    def send_far(k):
        return remote(pic.at[rows(k)], img.at[3, rows(k)], s2.at[k], r2.at[k], down)

    def forward_stage(k):
        return remote(stage.at[rows(k)], img.at[3, rows(k)], sg.at[k], r2.at[k], next_down)

    def forward_main(k):
        return remote(img.at[main, rows(k)], img.at[main, rows(k)], s3.at[k], r3.at[k], sibling)

    def send_part(k):
        return remote(grad.at[other, rows(k)], part.at[rows(k)], sp.at[k], rp.at[k], sibling)

    def send_first_back(k):
        return remote(grad.at[1, rows(k)], ret_far.at[rows(k)], sx.at[k], rx.at[k], first_back)

    to_across = jnp.where(b0, 1, 0)
    back = tuple(jnp.where(b0, x, y) for x, y in zip(across, up, strict=True))

    def send_main_back(k):
        return remote(
            grad.at[main, rows(k)], ret.at[to_across, rows(k)], sr.at[k], rr.at[to_across, k], back
        )

    def send_stage_back(k):
        return remote(grad.at[main, rows(k)], stage_back.at[rows(k)], sr.at[k], rb.at[k], next_up)

    def forward_stage_back(k):
        return remote(stage_back.at[rows(k)], ret.at[0, rows(k)], sb.at[k], rr.at[0, k], down)

    def get_back(which, k):
        return remote(grad.at[main, rows(k)], ret.at[which, rows(k)], sr.at[k], rr.at[which, k], back)

    def send_text(k):
        return remote(
            text_grad.at[rows(q * chunks + k)], text_ret.at[rows(k)], st.at[k], rt.at[k], partner
        )

    load_own = pltpu.make_async_copy(pic, img.at[0], load_sem.at[0])
    load_text = pltpu.make_async_copy(cap, text, load_sem.at[1])
    load_text.start()
    load_own.start()

    below = tuple(
        jnp.where(core == 0, x, jnp.where(low, y, z)) for x, y, z in zip(far, down, next_down, strict=True)
    )
    barrier = pltpu.get_barrier_semaphore()

    def greet(device, semaphore=barrier):
        pl.semaphore_signal(semaphore, inc=1, device_id=device, device_id_type=MESH)

    greet(below)
    greet(sibling)
    greet(partner)

    @pl.when(low)
    def _():
        greet(up)

    @pl.when(jnp.logical_not(low))
    def _():
        greet(down)

    @pl.when(a1 | b0)
    def _():
        greet(across)

    pl.semaphore_wait(barrier, jnp.where(a0, 3, jnp.where(b0, 4, jnp.where(a1, 5, 6))))

    @pl.when(core == 1)
    def _():
        greet(far, ready)

    @pl.when(b1)
    def _():
        greet(up, ready)
        greet(next_up, ready)

    @pl.loop(0, chunks)
    def _(k):
        @pl.when(b0)
        def _():
            send_main(k).start()

        @pl.when(a1 & (k < 2))
        def _():
            send_stage(k).start()

        @pl.when(core == 1)
        def _():
            send_first(k).start()

    @pl.when(core == 0)
    def _():
        pl.semaphore_wait(ready, 1)
        each(lambda k: send_first(k).start())

    scale, bias = scale_ref[0], bias_ref[0]
    load_text.wait()
    high, lower = halves(text[...])
    t_high[...] = high
    t_low[...] = lower
    tt_high[...] = high.T
    tt_low[...] = lower.T
    text_grad[...] = jnp.zeros_like(text_grad)
    load_own.wait()

    def score(slot, k, size):
        i_high, i_low = halves(img[slot, rows(k, size)])
        both = dot(jnp.concatenate([i_high, i_low], 0), tt_high[...])
        logits = scale * (both[:size] + both[size:] + dot(i_high, tt_low[...])) + bias
        row = lax.broadcasted_iota(jnp.int32, logits.shape, 0) + jnp.where(slot == 0, p * half + k * size, words)
        sign = jnp.where(row == lax.broadcasted_iota(jnp.int32, logits.shape, 1), -1.0, 1.0)
        coef = sign * jax.nn.sigmoid(sign * logits)
        c_high, c_low = halves(scale * coef)
        both = dot(jnp.concatenate([c_high, c_low], 0), t_high[...])
        grad[slot, rows(k, size)] = both[:size] + both[size:] + dot(c_high, t_low[...])
        text_grad[...] += lax.dot_general(
            jnp.concatenate([c_high, c_low, c_high], 0),
            jnp.concatenate([i_high, i_high, i_low], 0),
            (((0,), (0,)), ((), ())),
            preferred_element_type=F32,
        )

    def pass_on(k):
        @pl.when(a1 | b0)
        def _():
            send_first(k).wait_recv()

        @pl.when(a1 | (b0 & (k < 2)))
        def _():
            forward_first(k).start()

        @pl.when((b1 & (k == 0)) | (a1 & (k == 3)))
        def _():
            pl.semaphore_wait(ready, 1)

        @pl.when(b1 & (k < 2))
        def _():
            send_stage(k).wait_recv()
            forward_stage(k).start()

        @pl.when((core == 1) & (k == 3))
        def _():
            for u in (2, 3):
                send_far(u).start()

    def arrives(slot, k):
        @pl.when((slot == 1) & (a0 | b1))
        def _():
            send_first(k).wait_recv()

        @pl.when(slot == main)
        def _():
            send_main(k).wait_recv()
            forward_main(k).start()

        @pl.when(slot == other)
        def _():
            forward_main(k).wait_recv()

    def done(slot, k, count):
        @pl.when(slot == other)
        def _():
            for u in range(count):
                send_part(k + u).start()

    @pl.loop(0, 6)
    def _(j):
        slot = jnp.where(j < 4, j // 2 + j // 3, jnp.where(j == 5, 1, jnp.where(low, 2, 3)))
        part_at = jnp.where((j == 1) | (j == 5) | ((j == 4) & low), 1, 0)

        @pl.when((j > 0) & (j < 5))
        def _():
            pass_on(j - 1)

        for u in range(2):
            arrives(slot, 2 * part_at + u)
        score(slot, part_at, 2 * CHUNK)
        done(slot, 2 * part_at, 2)

        @pl.when((slot == 1) & ((core == 0) | (b1 & (j == 2))))
        def _():
            for u in range(2):
                send_first_back(2 * part_at + u).start()

    def give_back(k):
        send_part(k).wait_recv()
        grad[main, rows(k)] += part[rows(k)]

        @pl.when(b1)
        def _():
            send_stage_back(k).start()

        @pl.when(jnp.logical_not(b1))
        def _():
            send_main_back(k).start()

    def give_back_two(first):
        for u in range(2):
            give_back(first + u)

    @pl.when(jnp.logical_not(low))
    def _():
        give_back_two(0)

    @pl.loop(0, chunks)
    def _(j):
        slot = jnp.where(low, 3, 2 + lax.rem(j, 2))
        k = jnp.where(low, j, 2 + j // 2)
        arrives(slot, k)
        score(slot, k, CHUNK)
        done(slot, k, 1)

        @pl.when(low & (j == 2))
        def _():
            give_back_two(0)

        @pl.when(a0 & (j == 2))
        def _():
            give_back_two(2)

    each(lambda k: send_text(k).start())

    @pl.when(jnp.logical_not(a0))
    def _():
        give_back_two(2)

    @pl.when(b1)
    def _():
        def step(k):
            send_stage_back(k).wait_recv()
            forward_stage_back(k).start()

        for u in (2, 3):
            send_first_back(u).start()
        each(step)

    @pl.when(a1)
    def _():
        def chain(k):
            get_back(1, k).wait_recv()
            grad[1, rows(k)] += ret[1, rows(k)]
            send_first_back(k).start()

        each(chain)

    @pl.loop(0, chunks)
    def _(k):
        @pl.when(jnp.logical_not(a0))
        def _():
            get_back(0, k).wait_recv()
            grad[0, rows(k)] += ret[0, rows(k)]

        send_text(k).wait_recv()
        text_grad[rows(p * chunks + k)] += text_ret[rows(k)]
        pltpu.make_async_copy(
            text_grad.at[rows(p * chunks + k)], text_out.at[rows(k)], out_sem.at[0, k]
        ).start()
        send_first_back(k).wait_recv()
        grad[0, rows(k)] += ret_far[rows(k)]
        pltpu.make_async_copy(grad.at[0, rows(k)], image_out.at[rows(k)], out_sem.at[1, k]).start()

    @pl.loop(0, chunks)
    def _(k):
        send_first(k).wait_send()

        @pl.when(b0)
        def _():
            send_main(k).wait_send()

        @pl.when(a1 | (b1 & (k > 1)))
        def _():
            send_stage(k).wait_send()

        @pl.when(b1 & (k < 2))
        def _():
            forward_stage(k).wait_send()

        @pl.when(b1)
        def _():
            forward_stage_back(k).wait_send()

        @pl.when(a1 | (b0 & (k < 2)))
        def _():
            forward_first(k).wait_send()

        forward_main(k).wait_send()
        send_part(k).wait_send()
        send_main_back(k).wait_send()
        send_first_back(k).wait_send()
        send_text(k).wait_send()
        pltpu.make_async_copy(
            text_grad.at[rows(p * chunks + k)], text_out.at[rows(k)], out_sem.at[0, k]
        ).wait()
        pltpu.make_async_copy(grad.at[0, rows(k)], image_out.at[rows(k)], out_sem.at[1, k]).wait()


def solution(mesh):
    n = mesh.shape["dp"]

    def shards(picture_features, caption_features, sharpness_factor, score_intercept):
        half, width = picture_features.shape
        words = caption_features.shape[0]
        chunks = half // CHUNK
        dma = pltpu.SemaphoreType.DMA
        return pl.pallas_call(
            functools.partial(kernel, n),
            name="window_grads",
            out_shape=[jax.ShapeDtypeStruct((half, width), F32)] * 2,
            in_specs=[pl.BlockSpec(memory_space=pltpu.SMEM)] * 2 + [pl.BlockSpec(memory_space=pl.ANY)] * 2,
            out_specs=[pl.BlockSpec(memory_space=pl.ANY)] * 2,
            scratch_shapes=[
                pltpu.VMEM((4, half, width), F32),
                pltpu.VMEM((words, width), F32),
                pltpu.VMEM((words, width), BF16),
                pltpu.VMEM((words, width), BF16),
                pltpu.VMEM((width, words), BF16),
                pltpu.VMEM((width, words), BF16),
                pltpu.VMEM((4, half, width), F32),
                pltpu.VMEM((words, width), F32),
                pltpu.VMEM((half, width), F32),
                pltpu.VMEM((2, half, width), F32),
                pltpu.VMEM((half, width), F32),
                pltpu.VMEM((half, width), F32),
                pltpu.VMEM((half, width), F32),
                pltpu.VMEM((half, width), F32),
                dma((2,)),
                dma((2, chunks)),
            ]
            + [dma((chunks,))] * 16
            + [dma((2, chunks)), dma((chunks,)), dma((chunks,)), pltpu.SemaphoreType.REGULAR],
            compiler_params=pltpu.CompilerParams(
                collective_id=0, has_side_effects=True, vmem_limit_bytes=62 * 2**20
            ),
            cost_estimate=pl.CostEstimate(
                flops=4 * 3 * 2 * half * words * width, bytes_accessed=4 * width * (3 * half + words), transcendentals=0
            ),
        )(sharpness_factor, score_intercept, picture_features, caption_features)

    return jax.shard_map(
        shards,
        mesh=mesh,
        in_specs=(P(("dp", "pair"), None), P("dp", None), P(), P()),
        out_specs=(P(("dp", "pair"), None), P(("dp", "pair"), None)),
        check_vma=False,
    )
```

```python
import functools

import jax
import jax.numpy as jnp
from jax import lax
from jax.experimental import pallas as pl
from jax.experimental.pallas import tpu as pltpu
from jax.sharding import PartitionSpec as P

MESH = pl.DeviceIdType.MESH
F32, BF16 = jnp.float32, jnp.bfloat16
CHUNK = 64


def halves(value):
    high = value.astype(BF16)
    return high, (value - high.astype(F32)).astype(BF16)


def dot(a, b):
    return jnp.dot(a, b, preferred_element_type=F32)


def kernel(
    n, scale_ref, bias_ref, pic, cap, image_out, text_out,
    img, text, t_high, t_low, tt_high, tt_low, grad, text_grad,
    part, ret, ret_far, text_ret, stage, stage_back,
    load_sem, out_sem, s1, s2, s3, sf, sp, sr, sx, st, sg, sb, r1, r2, r3, rp, rg, rb, rr, rx, rt, ready, clear,
):
    dp, p = lax.axis_index("dp"), lax.axis_index("pair")
    half, words = pic.shape[0], cap.shape[0]
    chunks = half // CHUNK
    core = lax.rem(dp, 2)
    low = lax.rem(dp, 4) < 2
    a0 = low & (core == 0)
    a1 = low & (core == 1)
    b0 = jnp.logical_not(low) & (core == 0)
    b1 = jnp.logical_not(low) & (core == 1)

    def there(step, row):
        return (lax.rem(dp + step + n, n), row)

    q = 1 - p
    sibling = there(1 - 2 * core, p)
    down, up = there(-2, q), there(2, q)
    across = there(jnp.where(core == 1, 1, -1), q)
    far = there(jnp.where(core == 1, 3, -3), p)
    first_to = there(jnp.where(core == 1, -1, -3), p)
    first_back = there(jnp.where(core == 1, 3, 1), p)
    partner = (dp, q)
    main, other = 2 + core, 3 - core
    next_up, next_down = there(4, p), there(-4, p)

    def rows(k, size=CHUNK):
        return pl.ds(pl.multiple_of(k * size, size), size)

    def remote(src, dst, send, recv, device):
        return pltpu.make_async_remote_copy(
            src_ref=src, dst_ref=dst, send_sem=send, recv_sem=recv, device_id=device, device_id_type=MESH
        )

    def each(body, count=chunks):
        def run(k, _):
            body(k)
            return 0

        lax.fori_loop(0, count, run, 0)

    def send_main(k):
        return remote(pic.at[rows(k)], img.at[main, rows(k)], s2.at[k], r2.at[k], down)

    def send_first(k):
        return remote(pic.at[rows(k)], img.at[1, rows(k)], s1.at[k], r1.at[k], first_to)

    def forward_first(k):
        return remote(img.at[1, rows(k)], img.at[other, rows(k)], sf.at[k], r2.at[k], across)

    def send_stage(k):
        return remote(pic.at[rows(k)], stage.at[rows(k)], s2.at[k], rg.at[k], up)

    def send_far(k):
        return remote(pic.at[rows(k)], img.at[3, rows(k)], s2.at[k], r2.at[k], down)

    def forward_stage(k):
        return remote(stage.at[rows(k)], img.at[3, rows(k)], sg.at[k], r2.at[k], next_down)

    def forward_main(k):
        return remote(img.at[main, rows(k)], img.at[main, rows(k)], s3.at[k], r3.at[k], sibling)

    def send_part(k):
        return remote(grad.at[other, rows(k)], part.at[rows(k)], sp.at[k], rp.at[k], sibling)

    def send_first_back(k):
        return remote(grad.at[1, rows(k)], ret_far.at[rows(k)], sx.at[k], rx.at[k], first_back)

    to_across = jnp.where(b0, 1, 0)
    back = tuple(jnp.where(b0, x, y) for x, y in zip(across, up, strict=True))

    def send_main_back(k):
        return remote(
            grad.at[main, rows(k)], ret.at[to_across, rows(k)], sr.at[k], rr.at[to_across, k], back
        )

    def send_stage_back(k):
        return remote(grad.at[main, rows(k)], stage_back.at[rows(k)], sr.at[k], rb.at[k], next_up)

    def forward_stage_back(k):
        return remote(stage_back.at[rows(k)], ret.at[0, rows(k)], sb.at[k], rr.at[0, k], down)

    def get_back(which, k):
        return remote(grad.at[main, rows(k)], ret.at[which, rows(k)], sr.at[k], rr.at[which, k], back)

    def send_text(k):
        return remote(
            text_grad.at[rows(q * chunks + k)], text_ret.at[rows(k)], st.at[k], rt.at[k], partner
        )

    load_own = pltpu.make_async_copy(pic, img.at[0], load_sem.at[0])
    load_text = pltpu.make_async_copy(cap, text, load_sem.at[1])
    load_text.start()
    load_own.start()

    below = tuple(
        jnp.where(core == 0, x, jnp.where(low, y, z)) for x, y, z in zip(far, down, next_down, strict=True)
    )
    barrier = pltpu.get_barrier_semaphore()

    def greet(device, semaphore=barrier):
        pl.semaphore_signal(semaphore, inc=1, device_id=device, device_id_type=MESH)

    greet(below)
    greet(sibling)
    greet(partner)

    @pl.when(low)
    def _():
        greet(up)

    @pl.when(jnp.logical_not(low))
    def _():
        greet(down)

    @pl.when(a1 | b0)
    def _():
        greet(across)

    pl.semaphore_wait(barrier, jnp.where(a0, 3, jnp.where(b0, 4, jnp.where(a1, 5, 6))))

    @pl.when(core == 1)
    def _():
        greet(far, ready)

    @pl.when(b1)
    def _():
        greet(up, ready)
        greet(next_up, ready)

    @pl.loop(0, chunks)
    def _(k):
        @pl.when(b0)
        def _():
            send_main(k).start()

        @pl.when(a1 & (k < 2))
        def _():
            send_stage(k).start()

        @pl.when(core == 1)
        def _():
            send_first(k).start()

    @pl.when(core == 0)
    def _():
        pl.semaphore_wait(ready, 1)
        each(lambda k: send_first(k).start())

    scale, bias = scale_ref[0], bias_ref[0]
    load_text.wait()
    high, lower = halves(text[...])
    t_high[...] = high
    t_low[...] = lower
    tt_high[...] = high.T
    tt_low[...] = lower.T
    text_grad[...] = jnp.zeros_like(text_grad)
    load_own.wait()

    def score(slot, k, size):
        i_high, i_low = halves(img[slot, rows(k, size)])
        both = dot(jnp.concatenate([i_high, i_low], 0), tt_high[...])
        logits = scale * (both[:size] + both[size:] + dot(i_high, tt_low[...])) + bias
        row = lax.broadcasted_iota(jnp.int32, logits.shape, 0) + jnp.where(slot == 0, p * half + k * size, words)
        sign = jnp.where(row == lax.broadcasted_iota(jnp.int32, logits.shape, 1), -1.0, 1.0)
        coef = sign * jax.nn.sigmoid(sign * logits)
        c_high, c_low = halves(scale * coef)
        both = dot(jnp.concatenate([c_high, c_low], 0), t_high[...])
        grad[slot, rows(k, size)] = both[:size] + both[size:] + dot(c_high, t_low[...])
        text_grad[...] += lax.dot_general(
            jnp.concatenate([c_high, c_low, c_high], 0),
            jnp.concatenate([i_high, i_high, i_low], 0),
            (((0,), (0,)), ((), ())),
            preferred_element_type=F32,
        )

    def pass_on(k):
        @pl.when(a1 | b0)
        def _():
            send_first(k).wait_recv()

        @pl.when(a1 | (b0 & (k < 2)))
        def _():
            forward_first(k).start()

        @pl.when((b1 & (k == 0)) | (a1 & (k == 3)))
        def _():
            pl.semaphore_wait(ready, 1)

        @pl.when(b1 & (k < 2))
        def _():
            send_stage(k).wait_recv()
            forward_stage(k).start()

        @pl.when((core == 1) & (k == 3))
        def _():
            for u in (2, 3):
                send_far(u).start()

    def arrives(slot, k):
        @pl.when((slot == 1) & (a0 | b1))
        def _():
            send_first(k).wait_recv()

        @pl.when(slot == main)
        def _():
            send_main(k).wait_recv()
            forward_main(k).start()

        @pl.when(slot == other)
        def _():
            forward_main(k).wait_recv()

    def done(slot, k, count):
        @pl.when(slot == other)
        def _():
            for u in range(count):
                send_part(k + u).start()

    @pl.loop(0, 6)
    def _(j):
        fifth = jnp.where(low, 2, jnp.where(core == 0, 1, 3))
        sixth = jnp.where(b0, 3, 1)
        slot = jnp.where(j < 4, j // 2 + j // 3, jnp.where(j == 4, fifth, sixth))
        part_at = jnp.where((j == 1) | ((j > 3) & (slot != 3)), 1, 0)

        @pl.when((j > 0) & (j < 5))
        def _():
            pass_on(j - 1)

        for u in range(2):
            arrives(slot, 2 * part_at + u)
        score(slot, part_at, 2 * CHUNK)
        done(slot, 2 * part_at, 2)

        @pl.when((slot == 1) & ((core == 0) | (b1 & (j == 2))))
        def _():
            for u in range(2):
                send_first_back(2 * part_at + u).start()

    def give_back(k):
        send_part(k).wait_recv()
        grad[main, rows(k)] += part[rows(k)]

        @pl.when(b1)
        def _():
            send_stage_back(k).start()

        @pl.when(jnp.logical_not(b1))
        def _():
            send_main_back(k).start()

    def stage_back_arrives(k):
        send_stage_back(k).wait_recv()
        forward_stage_back(k).start()

    def give_back_two(first):
        for u in range(2):
            give_back(first + u)

    @pl.when(b0)
    def _():
        give_back_two(0)

    def main_arrives(k):
        send_main(k).wait_recv()
        forward_main(k).start()

    @pl.loop(0, chunks)
    def _(j):
        slot = jnp.where(low, 3, jnp.where(lax.rem(j, 2) == 0, main, other))
        k = jnp.where(low, j, 2 + j // 2)

        @pl.when(low)
        def _():
            arrives(slot, k)

        @pl.when(jnp.logical_not(low) & (j < 2))
        def _():
            main_arrives(2 + j)

        @pl.when(jnp.logical_not(low) & (slot == other))
        def _():
            forward_main(k).wait_recv()

        score(slot, k, CHUNK)
        done(slot, k, 1)

        @pl.when(b1 & (j == 2))
        def _():
            stage_back_arrives(0)

        @pl.when((low & (j == 2)) | (b1 & (j == 0)))
        def _():
            give_back_two(0)

        @pl.when(a0 & (j == 2))
        def _():
            give_back_two(2)

    each(lambda k: send_text(k).start())

    @pl.when(jnp.logical_not(a0))
    def _():
        give_back_two(2)

    @pl.when(b0)
    def _():
        for u in (2, 3):
            send_main_back(u).wait_send()
        pl.semaphore_signal(clear, inc=1, device_id=sibling, device_id_type=MESH)

    @pl.when(b1)
    def _():
        for u in (2, 3):
            send_first_back(u).start()
        pl.semaphore_wait(clear, 1)
        for u in (1, 2, 3):
            stage_back_arrives(u)

    @pl.when(a1)
    def _():
        def chain(k):
            get_back(1, k).wait_recv()
            grad[1, rows(k)] += ret[1, rows(k)]
            send_first_back(k).start()

        each(chain)

    @pl.loop(0, chunks)
    def _(k):
        @pl.when(jnp.logical_not(a0))
        def _():
            get_back(0, k).wait_recv()
            grad[0, rows(k)] += ret[0, rows(k)]

        send_text(k).wait_recv()
        text_grad[rows(p * chunks + k)] += text_ret[rows(k)]
        pltpu.make_async_copy(
            text_grad.at[rows(p * chunks + k)], text_out.at[rows(k)], out_sem.at[0, k]
        ).start()
        send_first_back(k).wait_recv()
        grad[0, rows(k)] += ret_far[rows(k)]
        pltpu.make_async_copy(grad.at[0, rows(k)], image_out.at[rows(k)], out_sem.at[1, k]).start()

    @pl.loop(0, chunks)
    def _(k):
        send_first(k).wait_send()

        @pl.when(b0)
        def _():
            send_main(k).wait_send()

        @pl.when(a1 | (b1 & (k > 1)))
        def _():
            send_stage(k).wait_send()

        @pl.when(b1 & (k < 2))
        def _():
            forward_stage(k).wait_send()

        @pl.when(b1)
        def _():
            forward_stage_back(k).wait_send()

        @pl.when(a1 | (b0 & (k < 2)))
        def _():
            forward_first(k).wait_send()

        forward_main(k).wait_send()
        send_part(k).wait_send()

        @pl.when(jnp.logical_not(b0 & (k > 1)))
        def _():
            send_main_back(k).wait_send()

        send_first_back(k).wait_send()
        send_text(k).wait_send()
        pltpu.make_async_copy(
            text_grad.at[rows(p * chunks + k)], text_out.at[rows(k)], out_sem.at[0, k]
        ).wait()
        pltpu.make_async_copy(grad.at[0, rows(k)], image_out.at[rows(k)], out_sem.at[1, k]).wait()


def solution(mesh):
    n = mesh.shape["dp"]

    def shards(picture_features, caption_features, sharpness_factor, score_intercept):
        half, width = picture_features.shape
        words = caption_features.shape[0]
        chunks = half // CHUNK
        dma = pltpu.SemaphoreType.DMA
        return pl.pallas_call(
            functools.partial(kernel, n),
            name="window_grads",
            out_shape=[jax.ShapeDtypeStruct((half, width), F32)] * 2,
            in_specs=[pl.BlockSpec(memory_space=pltpu.SMEM)] * 2 + [pl.BlockSpec(memory_space=pl.ANY)] * 2,
            out_specs=[pl.BlockSpec(memory_space=pl.ANY)] * 2,
            scratch_shapes=[
                pltpu.VMEM((4, half, width), F32),
                pltpu.VMEM((words, width), F32),
                pltpu.VMEM((words, width), BF16),
                pltpu.VMEM((words, width), BF16),
                pltpu.VMEM((width, words), BF16),
                pltpu.VMEM((width, words), BF16),
                pltpu.VMEM((4, half, width), F32),
                pltpu.VMEM((words, width), F32),
                pltpu.VMEM((half, width), F32),
                pltpu.VMEM((2, half, width), F32),
                pltpu.VMEM((half, width), F32),
                pltpu.VMEM((half, width), F32),
                pltpu.VMEM((half, width), F32),
                pltpu.VMEM((half, width), F32),
                dma((2,)),
                dma((2, chunks)),
            ]
            + [dma((chunks,))] * 16
            + [dma((2, chunks)), dma((chunks,)), dma((chunks,)), pltpu.SemaphoreType.REGULAR, pltpu.SemaphoreType.REGULAR],
            compiler_params=pltpu.CompilerParams(
                collective_id=0, has_side_effects=True, vmem_limit_bytes=62 * 2**20
            ),
            cost_estimate=pl.CostEstimate(
                flops=4 * 3 * 2 * half * words * width, bytes_accessed=4 * width * (3 * half + words), transcendentals=0
            ),
        )(sharpness_factor, score_intercept, picture_features, caption_features)

    return jax.shard_map(
        shards,
        mesh=mesh,
        in_specs=(P(("dp", "pair"), None), P("dp", None), P(), P()),
        out_specs=(P(("dp", "pair"), None), P(("dp", "pair"), None)),
        check_vma=False,
    )
```

```python
import functools

import jax
import jax.numpy as jnp
from jax import lax
from jax.experimental import pallas as pl
from jax.experimental.pallas import tpu as pltpu
from jax.sharding import PartitionSpec as P

MESH = pl.DeviceIdType.MESH
F32, BF16 = jnp.float32, jnp.bfloat16
CHUNK = 64
DEPTH = 16


def halves(value):
    high = value.astype(BF16)
    return high, (value - high.astype(F32)).astype(BF16)


def dot(a, b):
    return jnp.dot(a, b, preferred_element_type=F32)


def kernel(
    n, scale_ref, bias_ref, pic, cap, image_out, text_out,
    img, text, t_high, t_low, tt_high, tt_low, grad, text_grad,
    part, ret, ret_far, text_ret, stage, stage_back,
    load_sem, out_sem, s1, s2, s3, sf, sp, sr, sx, st, sg, sb, r1, r2, r3, rp, rg, rb, rr, rx, rt, ready, clear,
):
    dp, p = lax.axis_index("dp"), lax.axis_index("pair")
    half, words = pic.shape[0], cap.shape[0]
    chunks = half // CHUNK
    core = lax.rem(dp, 2)
    low = lax.rem(dp, 4) < 2
    a0 = low & (core == 0)
    a1 = low & (core == 1)
    b0 = jnp.logical_not(low) & (core == 0)
    b1 = jnp.logical_not(low) & (core == 1)
    edge = lax.rem(dp // 4, DEPTH) == 0

    def there(step, row):
        return (lax.rem(dp + step + n, n), row)

    q = 1 - p
    sibling = there(1 - 2 * core, p)
    down, up = there(-2, q), there(2, q)
    across = there(jnp.where(core == 1, 1, -1), q)
    far = there(jnp.where(core == 1, 3, -3), p)
    first_to = there(jnp.where(core == 1, -1, -3), p)
    first_back = there(jnp.where(core == 1, 3, 1), p)
    partner = (dp, q)
    main, other = 2 + core, 3 - core
    next_up, next_down = there(4, p), there(-4, p)

    def rows(k, size=CHUNK):
        return pl.ds(pl.multiple_of(k * size, size), size)

    def remote(src, dst, send, recv, device):
        return pltpu.make_async_remote_copy(
            src_ref=src, dst_ref=dst, send_sem=send, recv_sem=recv, device_id=device, device_id_type=MESH
        )

    def each(body, count=chunks):
        def run(k, _):
            body(k)
            return 0

        lax.fori_loop(0, count, run, 0)

    def send_main(k):
        return remote(pic.at[rows(k)], img.at[main, rows(k)], s2.at[k], r2.at[k], down)

    def send_first(k):
        return remote(pic.at[rows(k)], img.at[1, rows(k)], s1.at[k], r1.at[k], first_to)

    def forward_first(k):
        return remote(img.at[1, rows(k)], img.at[other, rows(k)], sf.at[k], r2.at[k], across)

    def send_stage(k):
        return remote(pic.at[rows(k)], stage.at[rows(k)], s2.at[k], rg.at[k], up)

    def send_far(k):
        return remote(pic.at[rows(k)], img.at[3, rows(k)], s2.at[k], r2.at[k], down)

    def forward_stage(k):
        return remote(stage.at[rows(k)], img.at[3, rows(k)], sg.at[k], r2.at[k], next_down)

    def forward_main(k):
        return remote(img.at[main, rows(k)], img.at[main, rows(k)], s3.at[k], r3.at[k], sibling)

    def send_part(k):
        return remote(grad.at[other, rows(k)], part.at[rows(k)], sp.at[k], rp.at[k], sibling)

    def send_first_back(k):
        return remote(grad.at[1, rows(k)], ret_far.at[rows(k)], sx.at[k], rx.at[k], first_back)

    to_across = jnp.where(b0, 1, 0)
    back = tuple(jnp.where(b0, x, y) for x, y in zip(across, up, strict=True))

    def send_main_back(k):
        return remote(
            grad.at[main, rows(k)], ret.at[to_across, rows(k)], sr.at[k], rr.at[to_across, k], back
        )

    def send_stage_back(k):
        return remote(grad.at[main, rows(k)], stage_back.at[rows(k)], sr.at[k], rb.at[k], next_up)

    def forward_stage_back(k):
        return remote(stage_back.at[rows(k)], ret.at[0, rows(k)], sb.at[k], rr.at[0, k], down)

    def get_back(which, k):
        return remote(grad.at[main, rows(k)], ret.at[which, rows(k)], sr.at[k], rr.at[which, k], back)

    def send_text(k):
        return remote(
            text_grad.at[rows(q * chunks + k)], text_ret.at[rows(k)], st.at[k], rt.at[k], partner
        )

    load_own = pltpu.make_async_copy(pic, img.at[0], load_sem.at[0])
    load_text = pltpu.make_async_copy(cap, text, load_sem.at[1])
    load_text.start()
    load_own.start()

    below = tuple(
        jnp.where(core == 0, x, jnp.where(low, y, z)) for x, y, z in zip(far, down, next_down, strict=True)
    )
    barrier = pltpu.get_barrier_semaphore()

    def greet(device, semaphore=barrier):
        pl.semaphore_signal(semaphore, inc=1, device_id=device, device_id_type=MESH)

    greet(below)
    greet(sibling)
    greet(partner)

    @pl.when(low)
    def _():
        greet(up)

    @pl.when(jnp.logical_not(low))
    def _():
        greet(down)

    @pl.when(a1 | b0)
    def _():
        greet(across)

    pl.semaphore_wait(barrier, jnp.where(a0, 3, jnp.where(b0, 4, jnp.where(a1, 5, 6))))

    @pl.when(core == 1)
    def _():
        greet(far, ready)

    @pl.when(b1)
    def _():
        greet(up, ready)
        greet(next_up, ready)

    @pl.loop(0, chunks)
    def _(k):
        @pl.when(b0)
        def _():
            send_main(k).start()

        @pl.when(a1 & (k < 2))
        def _():
            send_stage(k).start()

        @pl.when(core == 1)
        def _():
            send_first(k).start()

    def send_below():
        pl.semaphore_wait(ready, 1)
        each(lambda k: send_first(k).start())

    pl.when((core == 0) & jnp.logical_not(edge))(send_below)

    scale, bias = scale_ref[0], bias_ref[0]
    load_text.wait()
    high, lower = halves(text[...])
    t_high[...] = high
    t_low[...] = lower
    tt_high[...] = high.T
    tt_low[...] = lower.T
    text_grad[...] = jnp.zeros_like(text_grad)
    load_own.wait()

    def score(slot, k, size):
        i_high, i_low = halves(img[slot, rows(k, size)])
        both = dot(jnp.concatenate([i_high, i_low], 0), tt_high[...])
        logits = scale * (both[:size] + both[size:] + dot(i_high, tt_low[...])) + bias
        row = lax.broadcasted_iota(jnp.int32, logits.shape, 0) + jnp.where(slot == 0, p * half + k * size, words)
        sign = jnp.where(row == lax.broadcasted_iota(jnp.int32, logits.shape, 1), -1.0, 1.0)
        coef = sign * jax.nn.sigmoid(sign * logits)
        c_high, c_low = halves(scale * coef)
        both = dot(jnp.concatenate([c_high, c_low], 0), t_high[...])
        grad[slot, rows(k, size)] = both[:size] + both[size:] + dot(c_high, t_low[...])
        text_grad[...] += lax.dot_general(
            jnp.concatenate([c_high, c_low, c_high], 0),
            jnp.concatenate([i_high, i_high, i_low], 0),
            (((0,), (0,)), ((), ())),
            preferred_element_type=F32,
        )

    def send_last_two():
        @pl.when(a1)
        def _():
            pl.semaphore_wait(ready, 1)

        for u in (2, 3):
            send_far(u).start()

    def pass_on(k):
        @pl.when(a1 | b0)
        def _():
            send_first(k).wait_recv()

        @pl.when(a1 | (b0 & (k < 2)))
        def _():
            forward_first(k).start()

        @pl.when(b1 & (k == 0))
        def _():
            pl.semaphore_wait(ready, 1)

        @pl.when(b1 & (k < 2))
        def _():
            send_stage(k).wait_recv()
            forward_stage(k).start()

        pl.when((k == 3) & (b1 | (a1 & jnp.logical_not(edge))))(send_last_two)

    def arrives(slot, k):
        @pl.when((slot == 1) & (a0 | b1))
        def _():
            send_first(k).wait_recv()

        @pl.when(slot == main)
        def _():
            send_main(k).wait_recv()
            forward_main(k).start()

        @pl.when(slot == other)
        def _():
            forward_main(k).wait_recv()

    def done(slot, k, count):
        @pl.when(slot == other)
        def _():
            for u in range(count):
                send_part(k + u).start()

    @pl.loop(0, 6)
    def _(j):
        fifth = jnp.where(low, 2, jnp.where(core == 0, 1, 3))
        sixth = jnp.where(b0, 3, 1)
        slot = jnp.where(j < 4, j // 2 + j // 3, jnp.where(j == 4, fifth, sixth))
        part_at = jnp.where((j == 1) | ((j > 3) & (slot != 3)), 1, 0)

        @pl.when((j > 0) & (j < 5))
        def _():
            pass_on(j - 1)

        for u in range(2):
            arrives(slot, 2 * part_at + u)
        score(slot, part_at, 2 * CHUNK)
        done(slot, 2 * part_at, 2)
        pl.when((core == 0) & edge & (j == 2))(send_below)
        pl.when(a1 & edge & (j == 5))(send_last_two)

        @pl.when((slot == 1) & ((core == 0) | (b1 & (j == 2))))
        def _():
            for u in range(2):
                send_first_back(2 * part_at + u).start()

    def give_back(k):
        send_part(k).wait_recv()
        grad[main, rows(k)] += part[rows(k)]

        @pl.when(b1)
        def _():
            send_stage_back(k).start()

        @pl.when(jnp.logical_not(b1))
        def _():
            send_main_back(k).start()

    def stage_back_arrives(k):
        send_stage_back(k).wait_recv()
        forward_stage_back(k).start()

    def give_back_two(first):
        for u in range(2):
            give_back(first + u)

    @pl.when(b0)
    def _():
        give_back_two(0)

    def main_arrives(k):
        send_main(k).wait_recv()
        forward_main(k).start()

    @pl.loop(0, chunks)
    def _(j):
        slot = jnp.where(low, 3, jnp.where(lax.rem(j, 2) == 0, main, other))
        k = jnp.where(low, j, 2 + j // 2)

        @pl.when(low)
        def _():
            arrives(slot, k)

        @pl.when(jnp.logical_not(low) & (j == 0))
        def _():
            main_arrives(2)

        @pl.when((b1 & (j == 1)) | (b0 & (j == 2)))
        def _():
            main_arrives(3)

        @pl.when(jnp.logical_not(low) & (slot == other))
        def _():
            forward_main(k).wait_recv()

        score(slot, k, CHUNK)
        done(slot, k, 1)

        @pl.when(b1 & (j == 2) & jnp.logical_not(edge))
        def _():
            stage_back_arrives(0)

        @pl.when((low & (j == 2)) | (b1 & (j == 0)))
        def _():
            give_back_two(0)

        @pl.when(a0 & (j == 2))
        def _():
            give_back_two(2)

    each(lambda k: send_text(k).start())

    @pl.when(jnp.logical_not(a0))
    def _():
        give_back_two(2)

    @pl.when(b0)
    def _():
        for u in (2, 3):
            send_main_back(u).wait_send()
        pl.semaphore_signal(clear, inc=1, device_id=sibling, device_id_type=MESH)

    @pl.when(b1)
    def _():
        for u in (2, 3):
            send_first_back(u).start()
        pl.semaphore_wait(clear, 1)

        @pl.when(edge)
        def _():
            stage_back_arrives(0)

        for u in (1, 2, 3):
            stage_back_arrives(u)

    @pl.when(a1)
    def _():
        def chain(k):
            get_back(1, k).wait_recv()
            grad[1, rows(k)] += ret[1, rows(k)]
            send_first_back(k).start()

        each(chain)

    @pl.loop(0, chunks)
    def _(k):
        @pl.when(jnp.logical_not(a0))
        def _():
            get_back(0, k).wait_recv()
            grad[0, rows(k)] += ret[0, rows(k)]

        send_text(k).wait_recv()
        text_grad[rows(p * chunks + k)] += text_ret[rows(k)]
        pltpu.make_async_copy(
            text_grad.at[rows(p * chunks + k)], text_out.at[rows(k)], out_sem.at[0, k]
        ).start()
        send_first_back(k).wait_recv()
        grad[0, rows(k)] += ret_far[rows(k)]
        pltpu.make_async_copy(grad.at[0, rows(k)], image_out.at[rows(k)], out_sem.at[1, k]).start()

    @pl.loop(0, chunks)
    def _(k):
        send_first(k).wait_send()

        @pl.when(b0)
        def _():
            send_main(k).wait_send()

        @pl.when(a1 | (b1 & (k > 1)))
        def _():
            send_stage(k).wait_send()

        @pl.when(b1 & (k < 2))
        def _():
            forward_stage(k).wait_send()

        @pl.when(b1)
        def _():
            forward_stage_back(k).wait_send()

        @pl.when(a1 | (b0 & (k < 2)))
        def _():
            forward_first(k).wait_send()

        forward_main(k).wait_send()
        send_part(k).wait_send()

        @pl.when(jnp.logical_not(b0 & (k > 1)))
        def _():
            send_main_back(k).wait_send()

        send_first_back(k).wait_send()
        send_text(k).wait_send()
        pltpu.make_async_copy(
            text_grad.at[rows(p * chunks + k)], text_out.at[rows(k)], out_sem.at[0, k]
        ).wait()
        pltpu.make_async_copy(grad.at[0, rows(k)], image_out.at[rows(k)], out_sem.at[1, k]).wait()


def solution(mesh):
    n = mesh.shape["dp"]

    def shards(picture_features, caption_features, sharpness_factor, score_intercept):
        half, width = picture_features.shape
        words = caption_features.shape[0]
        chunks = half // CHUNK
        dma = pltpu.SemaphoreType.DMA
        return pl.pallas_call(
            functools.partial(kernel, n),
            name="window_grads",
            out_shape=[jax.ShapeDtypeStruct((half, width), F32)] * 2,
            in_specs=[pl.BlockSpec(memory_space=pltpu.SMEM)] * 2 + [pl.BlockSpec(memory_space=pl.ANY)] * 2,
            out_specs=[pl.BlockSpec(memory_space=pl.ANY)] * 2,
            scratch_shapes=[
                pltpu.VMEM((4, half, width), F32),
                pltpu.VMEM((words, width), F32),
                pltpu.VMEM((words, width), BF16),
                pltpu.VMEM((words, width), BF16),
                pltpu.VMEM((width, words), BF16),
                pltpu.VMEM((width, words), BF16),
                pltpu.VMEM((4, half, width), F32),
                pltpu.VMEM((words, width), F32),
                pltpu.VMEM((half, width), F32),
                pltpu.VMEM((2, half, width), F32),
                pltpu.VMEM((half, width), F32),
                pltpu.VMEM((half, width), F32),
                pltpu.VMEM((half, width), F32),
                pltpu.VMEM((half, width), F32),
                dma((2,)),
                dma((2, chunks)),
            ]
            + [dma((chunks,))] * 16
            + [dma((2, chunks)), dma((chunks,)), dma((chunks,)), pltpu.SemaphoreType.REGULAR, pltpu.SemaphoreType.REGULAR],
            compiler_params=pltpu.CompilerParams(
                collective_id=0, has_side_effects=True, vmem_limit_bytes=51 * 2**20
            ),
            cost_estimate=pl.CostEstimate(
                flops=4 * 3 * 2 * half * words * width, bytes_accessed=4 * width * (3 * half + words), transcendentals=0
            ),
        )(sharpness_factor, score_intercept, picture_features, caption_features)

    return jax.shard_map(
        shards,
        mesh=mesh,
        in_specs=(P(("dp", "pair"), None), P("dp", None), P(), P()),
        out_specs=(P(("dp", "pair"), None), P(("dp", "pair"), None)),
        check_vma=False,
    )
```

```python
import functools

import jax
import jax.numpy as jnp
from jax import lax
from jax.experimental import pallas as pl
from jax.experimental.pallas import tpu as pltpu
from jax.sharding import PartitionSpec as P

MESH = pl.DeviceIdType.MESH
F32, BF16 = jnp.float32, jnp.bfloat16
CHUNK = 64
DEPTH = 16


def halves(value):
    high = value.astype(BF16)
    return high, (value - high.astype(F32)).astype(BF16)


def dot(a, b):
    return jnp.dot(a, b, preferred_element_type=F32)


def kernel(
    n, scale_ref, bias_ref, pic, cap, image_out, text_out,
    img, text, t_high, t_low, tt_high, tt_low, grad, text_grad,
    part, ret, ret_far, text_ret, stage, stage_back,
    load_sem, out_sem, s1, s2, s3, sf, sp, sr, sx, st, sg, sb, r1, r2, r3, rp, rg, rb, rr, rx, rt, ready, clear,
):
    dp, p = lax.axis_index("dp"), lax.axis_index("pair")
    half, words = pic.shape[0], cap.shape[0]
    chunks = half // CHUNK
    core = lax.rem(dp, 2)
    low = lax.rem(dp, 4) < 2
    a0 = low & (core == 0)
    a1 = low & (core == 1)
    b0 = jnp.logical_not(low) & (core == 0)
    b1 = jnp.logical_not(low) & (core == 1)
    edge = lax.rem(dp // 4, DEPTH) == 0

    def there(step, row):
        return (lax.rem(dp + step + n, n), row)

    q = 1 - p
    sibling = there(1 - 2 * core, p)
    down, up = there(-2, q), there(2, q)
    across = there(jnp.where(core == 1, 1, -1), q)
    far = there(jnp.where(core == 1, 3, -3), p)
    first_to = there(jnp.where(core == 1, -1, -3), p)
    first_back = there(jnp.where(core == 1, 3, 1), p)
    partner = (dp, q)
    main, other = 2 + core, 3 - core
    next_up, next_down = there(4, p), there(-4, p)

    def rows(k, size=CHUNK):
        return pl.ds(pl.multiple_of(k * size, size), size)

    def remote(src, dst, send, recv, device):
        return pltpu.make_async_remote_copy(
            src_ref=src, dst_ref=dst, send_sem=send, recv_sem=recv, device_id=device, device_id_type=MESH
        )

    def each(body, count=chunks):
        def run(k, _):
            body(k)
            return 0

        lax.fori_loop(0, count, run, 0)

    def send_main(k):
        return remote(pic.at[rows(k)], img.at[main, rows(k)], s2.at[k], r2.at[k], down)

    def send_first(k):
        return remote(pic.at[rows(k)], img.at[1, rows(k)], s1.at[k], r1.at[k], first_to)

    def forward_first(k):
        return remote(img.at[1, rows(k)], img.at[other, rows(k)], sf.at[k], r2.at[k], across)

    def send_stage(k):
        return remote(pic.at[rows(k)], stage.at[rows(k)], s2.at[k], rg.at[k], up)

    def send_far(k):
        return remote(pic.at[rows(k)], img.at[3, rows(k)], s2.at[k], r2.at[k], down)

    def forward_stage(k):
        return remote(stage.at[rows(k)], img.at[3, rows(k)], sg.at[k], r2.at[k], next_down)

    def forward_main(k):
        return remote(img.at[main, rows(k)], img.at[main, rows(k)], s3.at[k], r3.at[k], sibling)

    def send_part(k):
        return remote(grad.at[other, rows(k)], part.at[rows(k)], sp.at[k], rp.at[k], sibling)

    def send_first_back(k):
        return remote(grad.at[1, rows(k)], ret_far.at[rows(k)], sx.at[k], rx.at[k], first_back)

    to_across = jnp.where(b0, 1, 0)
    back = tuple(jnp.where(b0, x, y) for x, y in zip(across, up, strict=True))

    def send_main_back(k):
        return remote(
            grad.at[main, rows(k)], ret.at[to_across, rows(k)], sr.at[k], rr.at[to_across, k], back
        )

    def send_stage_back(k):
        return remote(grad.at[main, rows(k)], stage_back.at[rows(k)], sr.at[k], rb.at[k], next_up)

    def forward_stage_back(k):
        return remote(stage_back.at[rows(k)], ret.at[0, rows(k)], sb.at[k], rr.at[0, k], down)

    def get_back(which, k):
        return remote(grad.at[main, rows(k)], ret.at[which, rows(k)], sr.at[k], rr.at[which, k], back)

    def send_text(k):
        return remote(
            text_grad.at[rows(q * chunks + k)], text_ret.at[rows(k)], st.at[k], rt.at[k], partner
        )

    load_own = pltpu.make_async_copy(pic, img.at[0], load_sem.at[0])
    load_text = pltpu.make_async_copy(cap, text, load_sem.at[1])
    load_text.start()
    load_own.start()

    below = tuple(
        jnp.where(core == 0, x, jnp.where(low, y, z)) for x, y, z in zip(far, down, next_down, strict=True)
    )
    barrier = pltpu.get_barrier_semaphore()

    def greet(device, semaphore=barrier):
        pl.semaphore_signal(semaphore, inc=1, device_id=device, device_id_type=MESH)

    greet(below)
    greet(sibling)
    greet(partner)

    @pl.when(low)
    def _():
        greet(up)

    @pl.when(jnp.logical_not(low))
    def _():
        greet(down)

    @pl.when(a1 | b0)
    def _():
        greet(across)

    pl.semaphore_wait(barrier, jnp.where(a0, 3, jnp.where(b0, 4, jnp.where(a1, 5, 6))))

    @pl.when(core == 1)
    def _():
        greet(far, ready)

    @pl.when(b1)
    def _():
        greet(up, ready)
        greet(next_up, ready)

    @pl.loop(0, chunks)
    def _(k):
        @pl.when(b0)
        def _():
            send_main(k).start()

        @pl.when(a1 & (k < 2))
        def _():
            send_stage(k).start()

        @pl.when(core == 1)
        def _():
            send_first(k).start()

    def send_below():
        pl.semaphore_wait(ready, 1)
        each(lambda k: send_first(k).start())

    pl.when((core == 0) & jnp.logical_not(edge))(send_below)

    scale, bias = scale_ref[0], bias_ref[0]
    load_text.wait()
    high, lower = halves(text[...])
    t_high[...] = high
    t_low[...] = lower
    tt_high[...] = high.T
    tt_low[...] = lower.T
    text_grad[...] = jnp.zeros_like(text_grad)
    load_own.wait()

    def score(slot, k, size):
        i_high, i_low = halves(img[slot, rows(k, size)])
        both = dot(jnp.concatenate([i_high, i_low], 0), tt_high[...])
        logits = scale * (both[:size] + both[size:] + dot(i_high, tt_low[...])) + bias
        row = lax.broadcasted_iota(jnp.int32, logits.shape, 0) + jnp.where(slot == 0, p * half + k * size, words)
        sign = jnp.where(row == lax.broadcasted_iota(jnp.int32, logits.shape, 1), -1.0, 1.0)
        coef = sign * jax.nn.sigmoid(sign * logits)
        c_high, c_low = halves(scale * coef)
        both = dot(jnp.concatenate([c_high, c_low], 0), t_high[...])
        grad[slot, rows(k, size)] = both[:size] + both[size:] + dot(c_high, t_low[...])
        text_grad[...] += lax.dot_general(
            jnp.concatenate([c_high, c_low, c_high], 0),
            jnp.concatenate([i_high, i_high, i_low], 0),
            (((0,), (0,)), ((), ())),
            preferred_element_type=F32,
        )

    def send_last_two():
        pl.semaphore_wait(ready, 1)
        for u in (2, 3):
            send_far(u).start()

    def pass_on(k):
        @pl.when(a1 | b0)
        def _():
            send_first(k).wait_recv()

        @pl.when(a1 | b0)
        def _():
            forward_first(k).start()

        @pl.when(b1 & (k == 0))
        def _():
            pl.semaphore_wait(ready, 1)

        @pl.when(b1 & (k < 2))
        def _():
            send_stage(k).wait_recv()
            forward_stage(k).start()

        pl.when((k == 3) & a1 & jnp.logical_not(edge))(send_last_two)

    def arrives(slot, k):
        @pl.when((slot == 1) & (a0 | b1))
        def _():
            send_first(k).wait_recv()

        @pl.when(slot == main)
        def _():
            send_main(k).wait_recv()
            forward_main(k).start()

        @pl.when(slot == other)
        def _():
            forward_main(k).wait_recv()

    def done(slot, k, count):
        @pl.when(slot == other)
        def _():
            for u in range(count):
                send_part(k + u).start()

    @pl.loop(0, 6)
    def _(j):
        fifth = jnp.where(low, 2, jnp.where(core == 0, 1, 3))
        sixth = jnp.where(b0, 3, 1)
        slot = jnp.where(j < 4, j // 2 + j // 3, jnp.where(j == 4, fifth, sixth))
        part_at = jnp.where((j == 1) | ((j > 3) & (slot != 3)), 1, 0)

        @pl.when((j > 0) & (j < 5))
        def _():
            pass_on(j - 1)

        for u in range(2):
            arrives(slot, 2 * part_at + u)
        score(slot, part_at, 2 * CHUNK)
        done(slot, 2 * part_at, 2)
        pl.when((core == 0) & edge & (j == 2))(send_below)
        pl.when(a1 & edge & (j == 5))(send_last_two)

        @pl.when((slot == 1) & ((core == 0) | (b1 & (j == 2))))
        def _():
            for u in range(2):
                send_first_back(2 * part_at + u).start()

    def give_back(k):
        send_part(k).wait_recv()
        grad[main, rows(k)] += part[rows(k)]

        @pl.when(b1)
        def _():
            send_stage_back(k).start()

        @pl.when(jnp.logical_not(b1))
        def _():
            send_main_back(k).start()

    def stage_back_arrives(k):
        send_stage_back(k).wait_recv()
        forward_stage_back(k).start()

    def give_back_two(first):
        for u in range(2):
            give_back(first + u)

    @pl.when(b0)
    def _():
        give_back_two(0)

    def main_arrives(k):
        send_main(k).wait_recv()
        forward_main(k).start()

    @pl.loop(0, chunks)
    def _(j):
        slot = jnp.where(low, 3, jnp.where(lax.rem(j, 2) == 0, main, other))
        k = jnp.where(low, j, 2 + j // 2)

        @pl.when(low)
        def _():
            arrives(slot, k)

        @pl.when(jnp.logical_not(low) & (j == 0))
        def _():
            main_arrives(2)

        @pl.when((b1 & (j == 1)) | (b0 & (j == 2)))
        def _():
            main_arrives(3)

        @pl.when(jnp.logical_not(low) & (slot == other))
        def _():
            forward_main(k).wait_recv()

        score(slot, k, CHUNK)
        done(slot, k, 1)

        @pl.when(b1 & (j == 2) & jnp.logical_not(edge))
        def _():
            stage_back_arrives(0)

        @pl.when((low & (j == 2)) | (b1 & (j == 0)))
        def _():
            give_back_two(0)

        @pl.when(a0 & (j == 2))
        def _():
            give_back_two(2)

    each(lambda k: send_text(k).start())

    @pl.when(jnp.logical_not(a0))
    def _():
        give_back_two(2)

    @pl.when(b0)
    def _():
        for u in (2, 3):
            send_main_back(u).wait_send()
        pl.semaphore_signal(clear, inc=1, device_id=sibling, device_id_type=MESH)

    @pl.when(b1)
    def _():
        for u in (2, 3):
            send_first_back(u).start()
        pl.semaphore_wait(clear, 1)

        @pl.when(edge)
        def _():
            stage_back_arrives(0)

        for u in (1, 2, 3):
            stage_back_arrives(u)

    @pl.when(a1)
    def _():
        def chain(k):
            get_back(1, k).wait_recv()
            grad[1, rows(k)] += ret[1, rows(k)]
            send_first_back(k).start()

        each(chain)

    @pl.loop(0, chunks)
    def _(k):
        @pl.when(jnp.logical_not(a0))
        def _():
            get_back(0, k).wait_recv()
            grad[0, rows(k)] += ret[0, rows(k)]

        send_text(k).wait_recv()
        text_grad[rows(p * chunks + k)] += text_ret[rows(k)]
        pltpu.make_async_copy(
            text_grad.at[rows(p * chunks + k)], text_out.at[rows(k)], out_sem.at[0, k]
        ).start()
        send_first_back(k).wait_recv()
        grad[0, rows(k)] += ret_far[rows(k)]
        pltpu.make_async_copy(grad.at[0, rows(k)], image_out.at[rows(k)], out_sem.at[1, k]).start()

    @pl.loop(0, chunks)
    def _(k):
        send_first(k).wait_send()

        @pl.when(b0)
        def _():
            send_main(k).wait_send()

        @pl.when(a1)
        def _():
            send_stage(k).wait_send()

        @pl.when(b1 & (k < 2))
        def _():
            forward_stage(k).wait_send()

        @pl.when(b1)
        def _():
            forward_stage_back(k).wait_send()

        @pl.when(a1 | b0)
        def _():
            forward_first(k).wait_send()

        forward_main(k).wait_send()
        send_part(k).wait_send()

        @pl.when(jnp.logical_not(b0 & (k > 1)))
        def _():
            send_main_back(k).wait_send()

        send_first_back(k).wait_send()
        send_text(k).wait_send()
        pltpu.make_async_copy(
            text_grad.at[rows(p * chunks + k)], text_out.at[rows(k)], out_sem.at[0, k]
        ).wait()
        pltpu.make_async_copy(grad.at[0, rows(k)], image_out.at[rows(k)], out_sem.at[1, k]).wait()


def solution(mesh):
    n = mesh.shape["dp"]

    def shards(picture_features, caption_features, sharpness_factor, score_intercept):
        half, width = picture_features.shape
        words = caption_features.shape[0]
        chunks = half // CHUNK
        dma = pltpu.SemaphoreType.DMA
        return pl.pallas_call(
            functools.partial(kernel, n),
            name="window_grads",
            out_shape=[jax.ShapeDtypeStruct((half, width), F32)] * 2,
            in_specs=[pl.BlockSpec(memory_space=pltpu.SMEM)] * 2 + [pl.BlockSpec(memory_space=pl.ANY)] * 2,
            out_specs=[pl.BlockSpec(memory_space=pl.ANY)] * 2,
            scratch_shapes=[
                pltpu.VMEM((4, half, width), F32),
                pltpu.VMEM((words, width), F32),
                pltpu.VMEM((words, width), BF16),
                pltpu.VMEM((words, width), BF16),
                pltpu.VMEM((width, words), BF16),
                pltpu.VMEM((width, words), BF16),
                pltpu.VMEM((4, half, width), F32),
                pltpu.VMEM((words, width), F32),
                pltpu.VMEM((half, width), F32),
                pltpu.VMEM((2, half, width), F32),
                pltpu.VMEM((half, width), F32),
                pltpu.VMEM((half, width), F32),
                pltpu.VMEM((half, width), F32),
                pltpu.VMEM((half, width), F32),
                dma((2,)),
                dma((2, chunks)),
            ]
            + [dma((chunks,))] * 16
            + [dma((2, chunks)), dma((chunks,)), dma((chunks,)), pltpu.SemaphoreType.REGULAR, pltpu.SemaphoreType.REGULAR],
            compiler_params=pltpu.CompilerParams(
                collective_id=0, has_side_effects=True, vmem_limit_bytes=51 * 2**20
            ),
            cost_estimate=pl.CostEstimate(
                flops=4 * 3 * 2 * half * words * width, bytes_accessed=4 * width * (3 * half + words), transcendentals=0
            ),
        )(sharpness_factor, score_intercept, picture_features, caption_features)

    return jax.shard_map(
        shards,
        mesh=mesh,
        in_specs=(P(("dp", "pair"), None), P("dp", None), P(), P()),
        out_specs=(P(("dp", "pair"), None), P(("dp", "pair"), None)),
        check_vma=False,
    )
```
